128 devices in a mesh: tp: 4 (over y), ad: 32 (over x, z, core).
Axes of the slice: x: 4, y: 4, z: 4, core: 2. Of those that a mesh axis runs over, the one named last changes fastest.
Arguments:
- queries: bfloat16 [8192, 4096], P('ad', 'tp'), may hold values from -300 to 300
- key_cache: bfloat16 [8192, 128, 512], P('ad', None, 'tp'), may hold values from -4 to 4
- value_cache: bfloat16 [8192, 128, 512], P('ad', None, 'tp'), may hold values from -6 to 6
- new_key: bfloat16 [8192, 512], P('ad', 'tp'), may hold values from -6 to 6
- new_value: bfloat16 [8192, 512], P('ad', 'tp'), may hold values from -6 to 6
- lengths: int32 [8192], P('ad'), may hold values from 2 to 128, as said below
- out_weight: bfloat16 [4096, 8192], P('tp'), may hold values from -0.09375 to 0.09375
- shrink_weight: bfloat16 [4096, 16384], P('tp', 'ad'), may hold values from -0.09375 to 0.09375
- expand_weight: bfloat16 [16384, 8192], P('ad', 'tp'), may hold values from -0.75 to 0.75
- adapter_id: int32 [8192], P('ad'), may hold values from 0 to 255, as said below
- adapter_slot: int32 [256], replicated, may hold values from 0 to 255, as said below
Outputs:
- projected: bfloat16 [8192, 8192], P('ad', 'tp')
The draws below stay inside these ranges and needn't reach their ends.
Inputs may be any that keep to these rules, and one draw needn't show every extreme that they name: `adapter_id`: rows are grouped by adapter within the rows of one device. Owner of adapter a is adapter_slot[a] // 8. The rows of one device name at most 16 rows for each owner, and every device names exactly 16 rows for one common owner drawn from the seed. `adapter_slot`: each value once. `lengths`: some row of every device has 128.
All inputs are finite; a program needn't handle non-finite values.
Results may differ from the reference program's by a relative error of at most 0.011.
Values may be sent and summed in bfloat16 or wider, within the bound.
A program may use at most 128 MiB of HBM per device.

```python
import math
import jax
import jax.numpy as jnp
from jax import lax

D = 8192
HEADS = 32
KV_HEADS = 4
HEAD_DIM = 128
RANK = 64
ROWS_DEV = 256
CACHE = 128
ADP_DEV = 8
ROWS = 8192
ADAPTERS = 256
CAP = 16


def routing(key):
    owner_count = ADAPTERS // ADP_DEV
    permuted = jax.random.permutation(jax.random.fold_in(key, 3), ADAPTERS).astype(jnp.int32)
    adapter_at = jnp.argsort(permuted).astype(jnp.int32)
    hottest = jax.random.randint(jax.random.fold_in(key, 4), (), 0, owner_count).astype(jnp.int32)
    others = jnp.arange(owner_count - 1, dtype=jnp.int32)
    others = others + (others >= hottest).astype(jnp.int32)
    pool = jnp.repeat(others, CAP, total_repeat_length=(owner_count - 1) * CAP)
    block_keys = jax.random.split(jax.random.fold_in(key, 5), owner_count)
    picked = jax.vmap(lambda one_key: jax.random.permutation(one_key, pool)[:ROWS_DEV - CAP])(block_keys)
    owners = jnp.concatenate([jnp.full((owner_count, CAP), hottest, jnp.int32), picked.astype(jnp.int32)], axis=1)
    uniform_pick = jax.random.randint(jax.random.fold_in(key, 6), (owner_count, ROWS_DEV), 0, ADP_DEV).astype(jnp.int32)
    local_pick = uniform_pick * uniform_pick // ADP_DEV
    chosen = adapter_at[owners * ADP_DEV + local_pick]
    chosen = jnp.sort(chosen, axis=1).reshape(-1)
    return (chosen.astype(jnp.int32), permuted)


def draw_adapter_id(key, part):
    return routing(key)[0]


def draw_adapter_slot(key, part):
    return routing(key)[1]


def draw_lengths(key, part):
    filled = jax.random.randint(jax.random.fold_in(key, 8), (ROWS,), 2, CACHE + 1).astype(jnp.int32)
    return filled.at[::ROWS_DEV].set(CACHE)


def attention_pair(key):
    cached = jnp.clip(jax.random.normal(jax.random.fold_in(key, 21), (ROWS, CACHE, KV_HEADS * HEAD_DIM), jnp.float32), -4.0, 4.0)
    asked = jnp.clip(jax.random.normal(jax.random.fold_in(key, 22), (ROWS, HEADS * HEAD_DIM), jnp.float32), -6.0, 6.0)
    return (asked, cached)


def draw_queries(key, part):
    return attention_pair(key)[0].astype(jnp.bfloat16)


def draw_key_cache(key, part):
    return attention_pair(key)[1].astype(jnp.bfloat16)


def block_scale(key, shape, cuts, low, top_value):
    factor_of, own = 1.0, jax.random.fold_in(key, 6)
    for position, blocks in cuts:
        draws = jnp.exp(jax.random.uniform(jax.random.fold_in(own, position), (blocks,), jnp.float32, low / len(cuts), top_value / len(cuts)))
        factor_of = factor_of * jnp.repeat(draws, shape[position] // blocks).reshape([-1 if axis == position else 1 for axis in range(len(shape))])
    return factor_of


def centred(key, shape, scale, bound, shards=(), kind=jnp.bfloat16):
    factor_of = block_scale(key, shape, shards, -0.22, 0.18) if shards else 1.0
    values = jax.random.normal(key, shape, jnp.float32) * scale * factor_of
    return jnp.minimum(jnp.maximum(values, -bound), bound).astype(kind)


def setup_inputs(seed: int = 0) -> dict:
    splits = jax.random.split(jax.random.key(seed), 12)
    queries = draw_queries(jax.random.fold_in(splits[11], 71), 0)
    key_cache = draw_key_cache(jax.random.fold_in(splits[11], 71), 0)
    value_cache = centred(splits[2], (ROWS, CACHE, KV_HEADS * HEAD_DIM), 1.0, 6.0, ((0, 32), (2, 4)))
    new_key = centred(splits[3], (ROWS, KV_HEADS * HEAD_DIM), 1.0, 6.0, ((0, 32), (1, 4)))
    new_value = centred(splits[4], (ROWS, KV_HEADS * HEAD_DIM), 1.0, 6.0, ((0, 32), (1, 4)))
    lengths = draw_lengths(jax.random.fold_in(splits[11], 71), 0)
    out_weight = centred(splits[6], (HEADS * HEAD_DIM, D), (HEADS * HEAD_DIM) ** -0.5, 0.09375, ((0, 4),))
    shrink_weight = centred(splits[7], (HEADS * HEAD_DIM, ADAPTERS * RANK), (HEADS * HEAD_DIM) ** -0.5, 0.09375, ((0, 4), (1, 32)))
    expand_weight = centred(splits[8], (ADAPTERS * RANK, D), RANK ** -0.5, 0.75, ((0, 32), (1, 4)))
    adapter_id = draw_adapter_id(jax.random.fold_in(splits[11], 71), 0)
    adapter_slot = draw_adapter_slot(jax.random.fold_in(splits[11], 71), 0)
    return dict(queries=queries, key_cache=key_cache, value_cache=value_cache, new_key=new_key, new_value=new_value, lengths=lengths, out_weight=out_weight, shrink_weight=shrink_weight, expand_weight=expand_weight, adapter_id=adapter_id, adapter_slot=adapter_slot)


def reference(queries, key_cache, value_cache, new_key, new_value, lengths, out_weight, shrink_weight, expand_weight, adapter_id, adapter_slot):
    row_count = queries.shape[0]
    group = HEADS // KV_HEADS
    scale = 1.0 / math.sqrt(HEAD_DIM)
    query_f = queries.astype(jnp.float32).reshape(row_count, KV_HEADS, group, HEAD_DIM)
    key_f = key_cache.astype(jnp.float32).reshape(row_count, CACHE, KV_HEADS, HEAD_DIM)
    value_f = value_cache.astype(jnp.float32).reshape(row_count, CACHE, KV_HEADS, HEAD_DIM)
    fresh_key = new_key.astype(jnp.float32).reshape(row_count, KV_HEADS, HEAD_DIM)
    fresh_value = new_value.astype(jnp.float32).reshape(row_count, KV_HEADS, HEAD_DIM)
    scores = jnp.einsum('rkgd,rckd->rkgc', query_f, key_f) * scale
    own = jnp.einsum('rkgd,rkd->rkg', query_f, fresh_key) * scale
    valid = jnp.arange(CACHE)[None, :] < lengths[:, None]
    valid = valid[:, None, None, :]
    scores = jnp.where(valid, scores, -jnp.inf)
    top = jnp.maximum(lax.optimization_barrier(jnp.max(scores, axis=-1)), own)
    expo = jnp.where(valid, jnp.exp(scores - top[..., None]), 0.0)
    own_expo = jnp.exp(own - top)
    total = lax.optimization_barrier(jnp.sum(expo, axis=-1)) + own_expo
    probs = (expo / total[..., None]).astype(jnp.bfloat16)
    own_prob = (own_expo / total).astype(jnp.bfloat16)
    attended = jnp.einsum('rkgc,rckd->rkgd', probs.astype(jnp.float32), value_f)
    attended = attended + own_prob.astype(jnp.float32)[..., None] * fresh_value[:, :, None, :]
    attended = attended.reshape(row_count, HEADS * HEAD_DIM).astype(jnp.bfloat16)
    base = jnp.dot(attended, out_weight, preferred_element_type=jnp.float32)
    slot = adapter_slot[adapter_id].astype(jnp.int32)

    def one_row(pair):
        features, place = pair
        start = (place * RANK).astype(jnp.int32)
        down = lax.dynamic_slice_in_dim(shrink_weight, start, RANK, 1)
        shrunk = jnp.dot(features, down, preferred_element_type=jnp.float32).astype(jnp.bfloat16)
        upward = lax.dynamic_slice_in_dim(expand_weight, start, RANK, 0)
        return jnp.dot(shrunk, upward, preferred_element_type=jnp.float32).astype(jnp.bfloat16)
    adapted = lax.map(one_row, (attended, slot))
    return (base + adapted.astype(jnp.float32)).astype(jnp.bfloat16)
```

```python
import math

import jax
import jax.numpy as jnp
from jax import lax
from jax.experimental import pallas as pl
from jax.experimental.pallas import tpu as pltpu
from jax.sharding import PartitionSpec as P

HEADS = 8
DIM = 128
RANK = 64
HELD = 8
ROWS = 256
SLOTS = 128
TP = 4
PEERS = 32
CAP = 16
WIDTH = HEADS * DIM
CHUNK = 2048
HALF = CHUNK // 2
AUX = 128
PACK = WIDTH + AUX
QUARTERS = 4
QPEERS = PEERS // QUARTERS
QROWS = QPEERS * CAP
KV_CHUNKS = 8
KV_ROWS = ROWS // KV_CHUNKS
BLOCK = 16
BF = jnp.bfloat16
F32 = jnp.float32
MESH = pl.DeviceIdType.MESH
NT = (((1,), (1,)), ((), ()))


def peer_offsets():
    quarters = [[] for _ in range(QUARTERS)]
    for dx in range(4):
        for dz in range(4):
            for dc in range(2):
                quarters[(dx + dz) % 2 + 2 * dc].append((dx, dz, dc))
    return [offset for quarter in quarters for offset in quarter]


OFFSETS = peer_offsets()


def iota(shape, axis):
    return lax.broadcasted_iota(jnp.int32, shape, axis)


def mm(a, b):
    return jnp.dot(a, b, preferred_element_type=F32)


def mm_nt(a, b):
    return lax.dot_general(a, b, NT, preferred_element_type=F32)


def kernel(
    q_hbm, k_hbm, v_hbm, nk_hbm, nv_hbm, w_hbm, shrink_hbm, expand_hbm, len_ref, id_ref, slot_ref,
    out_ref,
    q, kbuf, vbuf, nk, nv, wbuf, shrink, expand, qscr, oscr, att, sel, sel_t,
    packed, arrived, wid, ret, picks, ar_own, ar_send, ar_recv, rs_send, rs_recv, hold, own,
    sem_small, sem_k, sem_v, sem_w,
    s_fwd, r_fwd, s_back, r_back, s_ar, r_ar, s_rs, r_rs,
):
    me_t = lax.axis_index("tp")
    me_a = lax.axis_index("ad")
    me_x, me_z, me_c = me_a // 8, (me_a // 2) % 4, me_a % 2

    def ad_of(offset, sign):
        dx, dz, dc = offset
        x = (me_x + (sign * dx) % 4) % 4
        z = (me_z + (sign * dz) % 4) % 4
        return (x * 4 + z) * 2 + (me_c + dc) % 2

    def to_ad(offset, sign):
        return (me_t, ad_of(offset, sign))

    def to_tp(step):
        return ((me_t + step) % TP, me_a)

    def fetch(src, dst, sem):
        copy = pltpu.make_async_copy(src, dst, sem)
        copy.start()
        return copy

    small = [
        fetch(q_hbm, q, sem_small.at[0]),
        fetch(nk_hbm, nk, sem_small.at[1]),
        fetch(nv_hbm, nv, sem_small.at[2]),
    ]
    for i in range(KV_CHUNKS):
        rows = pl.ds(i * KV_ROWS, KV_ROWS)
        fetch(k_hbm.at[rows], kbuf.at[rows], sem_k.at[i])
        fetch(v_hbm.at[rows], vbuf.at[rows], sem_v.at[i])
    weights = []
    for i, step in enumerate((2, 1, 3, 0)):
        column = pl.multiple_of(((me_t + step) % TP) * CHUNK, CHUNK)
        weights.append(fetch(w_hbm.at[:, pl.ds(column, CHUNK)], wbuf.at[i], sem_w.at[i]))
        if i == 0:
            shrink_copy = fetch(shrink_hbm, shrink, sem_small.at[3])
            expand_copy = fetch(expand_hbm, expand, sem_small.at[4])

    barrier = pltpu.get_barrier_semaphore()
    for offset in OFFSETS[1:]:
        pl.semaphore_signal(barrier, inc=1, device_id=to_ad(offset, 1), device_id_type=MESH)
    for step in (1, 2, 3):
        pl.semaphore_signal(barrier, inc=1, device_id=to_tp(step), device_id_type=MESH)

    named = (iota((ROWS, ROWS), 0) == id_ref[...]).astype(F32).astype(BF)
    catalog = jnp.broadcast_to(slot_ref[...].astype(F32), (8, ROWS)).astype(BF)
    slot = mm(catalog, named)[0:1, :].astype(jnp.int32)
    owner = lax.shift_right_logical(slot, 3)
    local = jnp.bitwise_and(slot, HELD - 1)
    dx = jnp.bitwise_and(lax.shift_right_logical(owner, 3) - me_x, 3)
    dz = jnp.bitwise_and(lax.shift_right_logical(owner, 1) - me_z, 3)
    dc = jnp.bitwise_and(owner - me_c, 1)
    peer = jnp.bitwise_and(dx + dz, 1) * 8 + dc * 16 + dx * 2 + lax.shift_right_logical(dz, 1)
    hits = (iota((PEERS, ROWS), 0) == peer).astype(F32)
    before = (iota((ROWS, ROWS), 0) < iota((ROWS, ROWS), 1)).astype(F32).astype(BF)
    earlier = mm(hits.astype(BF), before)
    rank = jnp.sum(hits * earlier, axis=0, keepdims=True).astype(jnp.int32)
    place = peer * CAP + rank
    sel[...] = (iota((PEERS * CAP, ROWS), 0) == place).astype(F32).astype(BF)
    eye = (iota((ROWS, ROWS), 0) == iota((ROWS, ROWS), 1)).astype(F32).astype(BF)
    sel_t[...] = mm_nt(eye, sel[...]).astype(BF)
    local_hot = (iota((AUX, ROWS), 0) == local).astype(F32).astype(BF)
    aux = mm_nt(sel[...], local_hot).astype(BF)
    packed[:, :, WIDTH:] = aux.reshape(PEERS, CAP, AUX)

    for copy in small:
        copy.wait()
    scale = 1.0 / math.sqrt(DIM)
    group_rows = BLOCK * HEADS
    own_mask = iota((group_rows, BLOCK), 1) == iota((group_rows, BLOCK), 0) // HEADS
    lane = iota((HEADS, SLOTS), 1)
    blank = jnp.zeros((HEADS, DIM), F32)

    def attend(r0, part):
        rows = pl.ds(r0, BLOCK)
        qb = q[rows, :].astype(F32)
        for h in range(HEADS):
            qscr[part, pl.ds(h, BLOCK, stride=HEADS), :] = qb[:, h * DIM : (h + 1) * DIM]
        qv = qscr[part].astype(BF)
        fresh = mm_nt(qv, nk[rows, :]) * scale
        fresh = jnp.sum(jnp.where(own_mask, fresh, 0.0), axis=1, keepdims=True)
        pieces = []
        for i in range(BLOCK // 2):
            keys = kbuf[pl.ds(r0 + 2 * i, 2)].reshape(2 * SLOTS, DIM)
            s = mm_nt(qv[16 * i : 16 * i + 16], keys)
            for j in range(2):
                piece = s[8 * j : 8 * j + 8, SLOTS * j : SLOTS * (j + 1)] * scale
                pieces.append(jnp.where(lane < len_ref[r0 + 2 * i + j], piece, -jnp.inf))
        scores = jnp.concatenate(pieces, axis=0)
        top = jnp.maximum(jnp.max(scores, axis=1, keepdims=True), fresh)
        expo = jnp.exp(scores - top)
        fresh_expo = jnp.exp(fresh - top)
        total = jnp.sum(expo, axis=1, keepdims=True) + fresh_expo
        probs = expo / total
        fresh_prob = jnp.where(own_mask, fresh_expo / total, 0.0).astype(BF)
        mixed = []
        for i in range(BLOCK // 2):
            values = vbuf[pl.ds(r0 + 2 * i, 2)].reshape(2 * SLOTS, DIM)
            first = jnp.concatenate([probs[16 * i : 16 * i + 8], blank], axis=1)
            second = jnp.concatenate([blank, probs[16 * i + 8 : 16 * i + 16]], axis=1)
            mixed.append(mm(jnp.concatenate([first, second], axis=0).astype(BF), values))
        oscr[part] = jnp.concatenate(mixed, axis=0) + mm(fresh_prob, nv[rows, :])
        for h in range(HEADS):
            att[rows, h * DIM : (h + 1) * DIM] = oscr[part, pl.ds(h, BLOCK, stride=HEADS), :].astype(BF)

    def kv_step(i, carry):
        r0 = pl.multiple_of(i * KV_ROWS, KV_ROWS)
        rows = pl.ds(r0, KV_ROWS)
        pltpu.make_async_copy(k_hbm.at[rows], kbuf.at[rows], sem_k.at[i]).wait()
        pltpu.make_async_copy(v_hbm.at[rows], vbuf.at[rows], sem_v.at[i]).wait()
        for part in range(KV_ROWS // BLOCK):
            attend(pl.multiple_of(r0 + part * BLOCK, BLOCK), part)
        return carry

    lax.fori_loop(0, KV_CHUNKS, kv_step, 0)

    def send(src, dst, s, r, device):
        copy = pltpu.make_async_remote_copy(
            src_ref=src, dst_ref=dst, send_sem=s, recv_sem=r, device_id=device, device_id_type=MESH
        )
        copy.start()
        return copy

    packed[:, :, :WIDTH] = mm(sel[...], att[...]).astype(BF).reshape(PEERS, CAP, WIDTH)
    pl.semaphore_wait(barrier, PEERS - 1 + TP - 1)
    fwd = [None] * PEERS
    for k in range(1, PEERS):
        fwd[k] = send(packed.at[k], arrived.at[k], s_fwd.at[k], r_fwd.at[k], to_ad(OFFSETS[k], 1))
    arrived[0] = packed[0]

    tile = 512

    def ring(d, stage):
        return send(
            rs_send.at[d, stage], rs_recv.at[d, stage], s_rs.at[d, stage], r_rs.at[d, stage],
            to_tp(1 if d == 0 else 3),
        )

    def to_send(d, stage, start):
        def store(column, value):
            rs_send[d, stage, :, pl.ds(pl.multiple_of(column - start, tile), tile)] = value.astype(BF)

        return store

    def to_hold(d, start):
        def store(column, value):
            hold[d, :, pl.ds(pl.multiple_of(column - start, tile), tile)] = value

        return store

    def to_own(column, value):
        own[:, pl.ds(column, tile)] = value

    half = HALF // tile
    weights_done = [False] * TP

    def part(i, first, last, store):
        if not weights_done[i]:
            weights[i].wait()
            weights_done[i] = True

        def step(j, carry):
            column = pl.multiple_of(j * tile, tile)
            store(column, mm(att[...], wbuf[i, :, pl.ds(column, tile)]))
            return carry

        lax.fori_loop(first, last, step, 0)

    sent = [[None] * 3 for _ in range(2)]
    part(0, 0, half, to_send(0, 0, 0))
    sent[0][0] = ring(0, 0)
    part(0, half, 2 * half, to_send(1, 0, HALF))
    sent[1][0] = ring(1, 0)
    part(1, half, 2 * half, to_send(0, 1, HALF))
    part(1, 0, half, to_hold(0, 0))
    shrink_copy.wait()
    expand_copy.wait()

    spread_mask = (iota((AUX, HELD * RANK), 0) == iota((AUX, HELD * RANK), 1) // RANK).astype(F32).astype(BF)
    low = iota((QROWS // 2, 2 * RANK), 1) < RANK
    ar = [None] * QUARTERS
    back = [None] * PEERS

    def down(g):
        for k in range(g * QPEERS, (g + 1) * QPEERS):
            if k:
                fwd[k].wait_recv()
        rows = arrived[g * QPEERS : (g + 1) * QPEERS].reshape(QROWS, PACK)
        full = mm(rows[:, :WIDTH], shrink[...])
        pick = mm(rows[:, WIDTH:], spread_mask)
        picks[g] = pick.astype(BF)
        kept = jnp.where(pick > 0.5, full, 0.0)
        folded = sum(kept[:, i * 128 : (i + 1) * 128] for i in range(HELD * RANK // 128))
        both = folded + pltpu.roll(folded, RANK, 1)
        half_rows = jnp.where(low, both[: QROWS // 2], both[QROWS // 2 :])
        ar_own[g] = half_rows
        ar_send[g] = half_rows.astype(BF)
        ar[g] = [
            send(ar_send.at[g], ar_recv.at[g, d], s_ar.at[g, d], r_ar.at[g, d], to_tp(d + 1))
            for d in range(TP - 1)
        ]

    def up(g):
        for copy in ar[g]:
            copy.wait()
        total = ar_own[g]
        for d in range(TP - 1):
            total = total + ar_recv[g, d].astype(F32)
        other = pltpu.roll(total, RANK, 1)
        both = jnp.concatenate([jnp.where(low, total, other), jnp.where(low, other, total)], axis=0).astype(BF)
        spread = jnp.concatenate([both] * (HELD * RANK // 128), axis=1) * picks[g]
        peers = slice(g * QPEERS, (g + 1) * QPEERS)
        for j in range(CHUNK // tile):
            columns = slice(j * tile, (j + 1) * tile)
            wid[peers, :, columns] = mm(spread, expand[:, columns]).astype(BF).reshape(QPEERS, CAP, tile)
        for k in range(g * QPEERS, (g + 1) * QPEERS):
            if k:
                back[k] = send(wid.at[k], ret.at[k], s_back.at[k], r_back.at[k], to_ad(OFFSETS[k], -1))
            else:
                ret[0] = wid[0]

    down(0)
    part(2, 0, half, to_send(1, 1, 0))
    part(2, half, 2 * half, to_hold(1, HALF))
    down(1)
    part(3, 0, 2 * half, to_own)
    down(2)
    sent[0][1] = ring(0, 1)
    sent[1][1] = ring(1, 1)
    up(0)
    down(3)
    for d in range(2):
        sent[d][0].wait_recv()
        rs_send[d, 2] = (hold[d] + rs_recv[d, 0].astype(F32)).astype(BF)
        sent[d][2] = ring(d, 2)
    up(1)
    up(2)
    up(3)

    for d in range(2):
        sent[d][1].wait_recv()
    own[:, :HALF] += rs_recv[1, 1].astype(F32)
    own[:, HALF:] += rs_recv[0, 1].astype(F32)

    def returned(g, last=False):
        for k in range(g * QPEERS, (g + 1) * QPEERS):
            if k:
                back[k].wait_recv()
        chosen = sel_t[:, g * QROWS : (g + 1) * QROWS]
        for j in range(CHUNK // tile):
            columns = slice(j * tile, (j + 1) * tile)
            values = ret[g * QPEERS : (g + 1) * QPEERS, :, columns].reshape(QROWS, tile)
            value = own[:, columns] + mm(chosen, values)
            if last:
                out_ref[:, columns] = value.astype(BF)
            else:
                own[:, columns] = value

    returned(0)
    returned(1)
    for d in range(2):
        sent[d][2].wait_recv()
    own[:, :HALF] += rs_recv[0, 2].astype(F32)
    own[:, HALF:] += rs_recv[1, 2].astype(F32)
    returned(2)
    returned(3, last=True)

    for k in range(1, PEERS):
        fwd[k].wait_send()
        back[k].wait_send()
    for d in range(2):
        for stage in range(3):
            sent[d][stage].wait_send()


def shards(
    queries,
    key_cache,
    value_cache,
    new_key,
    new_value,
    lengths,
    out_weight,
    shrink_weight,
    expand_weight,
    adapter_id,
    adapter_slot,
):
    dma = pltpu.SemaphoreType.DMA
    hbm = pl.BlockSpec(memory_space=pl.ANY)
    vmem = pl.BlockSpec(memory_space=pltpu.VMEM)
    smem = pl.BlockSpec(memory_space=pltpu.SMEM)
    return pl.pallas_call(
        kernel,
        out_shape=jax.ShapeDtypeStruct((ROWS, CHUNK), BF),
        in_specs=[hbm] * 8 + [smem, vmem, vmem],
        out_specs=vmem,
        scratch_shapes=[
            pltpu.VMEM((ROWS, WIDTH), BF),
            pltpu.VMEM((ROWS, SLOTS, DIM), BF),
            pltpu.VMEM((ROWS, SLOTS, DIM), BF),
            pltpu.VMEM((ROWS, DIM), BF),
            pltpu.VMEM((ROWS, DIM), BF),
            pltpu.VMEM((TP, WIDTH, CHUNK), BF),
            pltpu.VMEM((WIDTH, HELD * RANK), BF),
            pltpu.VMEM((HELD * RANK, CHUNK), BF),
            pltpu.VMEM((KV_ROWS // BLOCK, BLOCK * HEADS, DIM), F32),
            pltpu.VMEM((KV_ROWS // BLOCK, BLOCK * HEADS, DIM), F32),
            pltpu.VMEM((ROWS, WIDTH), BF),
            pltpu.VMEM((PEERS * CAP, ROWS), BF),
            pltpu.VMEM((ROWS, PEERS * CAP), BF),
            pltpu.VMEM((PEERS, CAP, PACK), BF),
            pltpu.VMEM((PEERS, CAP, PACK), BF),
            pltpu.VMEM((PEERS, CAP, CHUNK), BF),
            pltpu.VMEM((PEERS, CAP, CHUNK), BF),
            pltpu.VMEM((QUARTERS, QROWS, HELD * RANK), BF),
            pltpu.VMEM((QUARTERS, QROWS // 2, 2 * RANK), F32),
            pltpu.VMEM((QUARTERS, QROWS // 2, 2 * RANK), BF),
            pltpu.VMEM((QUARTERS, TP - 1, QROWS // 2, 2 * RANK), BF),
            pltpu.VMEM((2, 3, ROWS, HALF), BF),
            pltpu.VMEM((2, 3, ROWS, HALF), BF),
            pltpu.VMEM((2, ROWS, HALF), F32),
            pltpu.VMEM((ROWS, CHUNK), F32),
            dma((5,)),
            dma((KV_CHUNKS,)),
            dma((KV_CHUNKS,)),
            dma((TP,)),
            dma((PEERS,)),
            dma((PEERS,)),
            dma((PEERS,)),
            dma((PEERS,)),
            dma((QUARTERS, TP - 1)),
            dma((QUARTERS, TP - 1)),
            dma((2, 3)),
            dma((2, 3)),
        ],
        compiler_params=pltpu.CompilerParams(
            collective_id=0, has_side_effects=True, vmem_limit_bytes=62 * 2**20
        ),
    )(
        queries,
        key_cache,
        value_cache,
        new_key,
        new_value,
        out_weight,
        shrink_weight,
        expand_weight,
        lengths,
        adapter_id.reshape(1, ROWS),
        adapter_slot.reshape(1, ROWS),
    )


def solution(mesh):
    in_specs = (
        P("ad", "tp"),
        P("ad", None, "tp"),
        P("ad", None, "tp"),
        P("ad", "tp"),
        P("ad", "tp"),
        P("ad"),
        P("tp", None),
        P("tp", "ad"),
        P("ad", "tp"),
        P("ad"),
        P(),
    )
    out_specs = P("ad", "tp")
    return jax.shard_map(shards, mesh=mesh, in_specs=in_specs, out_specs=out_specs, check_vma=False)
```

```python
import math

import jax
import jax.numpy as jnp
from jax import lax
from jax.experimental import pallas as pl
from jax.experimental.pallas import tpu as pltpu
from jax.sharding import PartitionSpec as P

HEADS = 8
DIM = 128
RANK = 64
HELD = 8
ROWS = 256
SLOTS = 128
TP = 4
PEERS = 32
CAP = 16
WIDTH = HEADS * DIM
CHUNK = 2048
HALF = CHUNK // 2
AUX = 128
QUARTERS = 4
QPEERS = PEERS // QUARTERS
QROWS = QPEERS * CAP
KV_CHUNKS = 8
KV_ROWS = ROWS // KV_CHUNKS
KV_AHEAD = 2
W_AFTER = 1
BLOCK = 16
BF = jnp.bfloat16
F32 = jnp.float32
MESH = pl.DeviceIdType.MESH
NT = (((1,), (1,)), ((), ()))


def peer_offsets():
    quarters = [[] for _ in range(QUARTERS)]
    for dx in range(4):
        for dz in range(4):
            for dc in range(2):
                quarters[(dx + dz) % 2 + 2 * dc].append((dx, dz, dc))
    return [offset for quarter in quarters for offset in quarter]


OFFSETS = peer_offsets()


def iota(shape, axis):
    return lax.broadcasted_iota(jnp.int32, shape, axis)


def mm(a, b):
    return jnp.dot(a, b, preferred_element_type=F32)


def mm_nt(a, b):
    return lax.dot_general(a, b, NT, preferred_element_type=F32)


def kernel(
    q_hbm, k_hbm, v_hbm, nk_hbm, nv_hbm, w_hbm, shrink_hbm, expand_hbm, len_hbm, id_hbm, slot_hbm,
    out_ref,
    len_ref, id_ref, slot_ref,
    q, kbuf, vbuf, nk, nv, wbuf, shrink, expand, qscr, oscr, att, sel, sel_t,
    packed, arrived, aux_send, aux_recv, wid, ret, picks, ar_own, ar_send, ar_recv, rs_send, rs_recv, hold, own,
    sem_small, sem_k, sem_v, sem_w,
    s_fwd, r_fwd, s_back, r_back, s_ar, r_ar, s_rs, r_rs, s_aux, r_aux,
):
    me_t = lax.axis_index("tp")
    me_a = lax.axis_index("ad")
    me_x, me_z, me_c = me_a // 8, (me_a // 2) % 4, me_a % 2

    def ad_of(offset, sign):
        dx, dz, dc = offset
        x = (me_x + (sign * dx) % 4) % 4
        z = (me_z + (sign * dz) % 4) % 4
        return (x * 4 + z) * 2 + (me_c + dc) % 2

    def to_ad(offset, sign):
        return (me_t, ad_of(offset, sign))

    def to_tp(step):
        return ((me_t + step) % TP, me_a)

    def fetch(src, dst, sem):
        copy = pltpu.make_async_copy(src, dst, sem)
        copy.start()
        return copy

    named_copies = [fetch(id_hbm, id_ref, sem_small.at[5]), fetch(slot_hbm, slot_ref, sem_small.at[6])]
    small = [
        fetch(len_hbm, len_ref, sem_small.at[7]),
        fetch(q_hbm, q, sem_small.at[0]),
        fetch(nk_hbm, nk, sem_small.at[1]),
        fetch(nv_hbm, nv, sem_small.at[2]),
    ]

    def kv_copies(i):
        rows = pl.ds(pl.multiple_of(i * KV_ROWS, KV_ROWS), KV_ROWS)
        return (
            pltpu.make_async_copy(k_hbm.at[rows], kbuf.at[rows], sem_k.at[i]),
            pltpu.make_async_copy(v_hbm.at[rows], vbuf.at[rows], sem_v.at[i]),
        )

    def start_kv(i):
        for copy in kv_copies(i):
            copy.start()

    for i in range(KV_AHEAD):
        start_kv(i)

    def weight_copy(i):
        column = pl.multiple_of(((me_t + (2, 1, 3, 0)[i]) % TP) * CHUNK, CHUNK)
        return pltpu.make_async_copy(w_hbm.at[:, pl.ds(column, CHUNK)], wbuf.at[i], sem_w.at[i])

    weights = [weight_copy(i) for i in range(TP)]
    shrink_copy = pltpu.make_async_copy(shrink_hbm, shrink, sem_small.at[3])
    expand_copy = pltpu.make_async_copy(expand_hbm, expand, sem_small.at[4])

    barrier = pltpu.get_barrier_semaphore()
    for offset in OFFSETS[1:]:
        pl.semaphore_signal(barrier, inc=1, device_id=to_ad(offset, 1), device_id_type=MESH)
    for step in (1, 2, 3):
        pl.semaphore_signal(barrier, inc=1, device_id=to_tp(step), device_id_type=MESH)

    for copy in named_copies:
        copy.wait()
    named = (iota((ROWS, ROWS), 0) == id_ref[...]).astype(F32).astype(BF)
    catalog = jnp.broadcast_to(slot_ref[...].astype(F32), (8, ROWS)).astype(BF)
    slot = mm(catalog, named)[0:1, :].astype(jnp.int32)
    owner = lax.shift_right_logical(slot, 3)
    local = jnp.bitwise_and(slot, HELD - 1)
    dx = jnp.bitwise_and(lax.shift_right_logical(owner, 3) - me_x, 3)
    dz = jnp.bitwise_and(lax.shift_right_logical(owner, 1) - me_z, 3)
    dc = jnp.bitwise_and(owner - me_c, 1)
    peer = jnp.bitwise_and(dx + dz, 1) * 8 + dc * 16 + dx * 2 + lax.shift_right_logical(dz, 1)
    hits = (iota((PEERS, ROWS), 0) == peer).astype(F32)
    before = (iota((ROWS, ROWS), 0) < iota((ROWS, ROWS), 1)).astype(F32).astype(BF)
    earlier = mm(hits.astype(BF), before)
    rank = jnp.sum(hits * earlier, axis=0, keepdims=True).astype(jnp.int32)
    place = peer * CAP + rank
    sel[...] = (iota((PEERS * CAP, ROWS), 0) == place).astype(F32).astype(BF)
    eye = (iota((ROWS, ROWS), 0) == iota((ROWS, ROWS), 1)).astype(F32).astype(BF)
    sel_t[...] = mm_nt(eye, sel[...]).astype(BF)
    local_hot = (iota((AUX, ROWS), 0) == local).astype(F32).astype(BF)
    aux = mm_nt(sel[...], local_hot).astype(BF)
    aux_send[...] = aux.reshape(PEERS, CAP, AUX)

    for copy in small:
        copy.wait()
    scale = 1.0 / math.sqrt(DIM)
    group_rows = BLOCK * HEADS
    own_mask = iota((group_rows, BLOCK), 1) == iota((group_rows, BLOCK), 0) // HEADS
    lane = iota((HEADS, SLOTS), 1)
    blank = jnp.zeros((HEADS, DIM), F32)

    def attend(r0, part):
        rows = pl.ds(r0, BLOCK)
        qb = q[rows, :].astype(F32)
        for h in range(HEADS):
            qscr[part, pl.ds(h, BLOCK, stride=HEADS), :] = qb[:, h * DIM : (h + 1) * DIM]
        qv = qscr[part].astype(BF)
        fresh = mm_nt(qv, nk[rows, :]) * scale
        fresh = jnp.sum(jnp.where(own_mask, fresh, 0.0), axis=1, keepdims=True)
        pieces = []
        for i in range(BLOCK // 2):
            keys = kbuf[pl.ds(r0 + 2 * i, 2)].reshape(2 * SLOTS, DIM)
            s = mm_nt(qv[16 * i : 16 * i + 16], keys)
            for j in range(2):
                piece = s[8 * j : 8 * j + 8, SLOTS * j : SLOTS * (j + 1)] * scale
                pieces.append(jnp.where(lane < len_ref[r0 + 2 * i + j], piece, -jnp.inf))
        scores = jnp.concatenate(pieces, axis=0)
        top = jnp.maximum(jnp.max(scores, axis=1, keepdims=True), fresh)
        expo = jnp.exp(scores - top)
        fresh_expo = jnp.exp(fresh - top)
        total = jnp.sum(expo, axis=1, keepdims=True) + fresh_expo
        probs = expo / total
        fresh_prob = jnp.where(own_mask, fresh_expo / total, 0.0).astype(BF)
        mixed = []
        for i in range(BLOCK // 2):
            values = vbuf[pl.ds(r0 + 2 * i, 2)].reshape(2 * SLOTS, DIM)
            first = jnp.concatenate([probs[16 * i : 16 * i + 8], blank], axis=1)
            second = jnp.concatenate([blank, probs[16 * i + 8 : 16 * i + 16]], axis=1)
            mixed.append(mm(jnp.concatenate([first, second], axis=0).astype(BF), values))
        oscr[part] = jnp.concatenate(mixed, axis=0) + mm(fresh_prob, nv[rows, :])
        for h in range(HEADS):
            att[rows, h * DIM : (h + 1) * DIM] = oscr[part, pl.ds(h, BLOCK, stride=HEADS), :].astype(BF)

    def send(src, dst, s, r, device):
        copy = pltpu.make_async_remote_copy(
            src_ref=src, dst_ref=dst, send_sem=s, recv_sem=r, device_id=device, device_id_type=MESH
        )
        copy.start()
        return copy

    tile = 512

    def ring(d, stage):
        return send(
            rs_send.at[d, stage], rs_recv.at[d, stage], s_rs.at[d, stage], r_rs.at[d, stage],
            to_tp(1 if d == 0 else 3),
        )

    def to_send(d, stage, start):
        def store(column, value):
            rs_send[d, stage, :, pl.ds(pl.multiple_of(column - start, tile), tile)] = value.astype(BF)

        return store

    def to_hold(d, start):
        def store(column, value):
            hold[d, :, pl.ds(pl.multiple_of(column - start, tile), tile)] = value

        return store

    def to_own(column, value):
        own[:, pl.ds(column, tile)] = value

    half = HALF // tile
    weights_done = [False] * TP

    def part(i, first, last, store):
        if not weights_done[i]:
            weights[i].wait()
            weights_done[i] = True

        def step(j, carry):
            column = pl.multiple_of(j * tile, tile)
            store(column, mm(att[...], wbuf[i, :, pl.ds(column, tile)]))
            return carry

        lax.fori_loop(first, last, step, 0)

    sent = [[None] * 3 for _ in range(2)]
    sent_half = [None, None]

    def ring_half(d, part_of):
        rows = pl.ds(part_of * (ROWS // 2), ROWS // 2)
        slot_of = 0 if part_of else 3
        return send(
            rs_send.at[d, 0, rows], rs_recv.at[d, 0, rows], s_rs.at[d, slot_of], r_rs.at[d, slot_of],
            to_tp(1 if d == 0 else 3),
        )

    def opposite(part_of):
        if part_of == 0:
            weights[0].wait()
        rows = slice(part_of * (ROWS // 2), (part_of + 1) * (ROWS // 2))
        for d in range(2):
            for j in range(half):
                columns = slice(j * tile, (j + 1) * tile)
                value = mm(att[rows, :], wbuf[0, :, d * HALF + j * tile : d * HALF + (j + 1) * tile])
                rs_send[d, 0, rows, columns] = value.astype(BF)
            copy = ring_half(d, part_of)
            if part_of:
                sent[d][0] = copy
            else:
                sent_half[d] = copy

    def kv_step(i, carry):
        for copy in kv_copies(i):
            copy.wait()

        @pl.when(i < KV_CHUNKS - KV_AHEAD)
        def _():
            start_kv(i + KV_AHEAD)

        @pl.when(i == W_AFTER)
        def _():
            weights[0].start()

        r0 = pl.multiple_of(i * KV_ROWS, KV_ROWS)
        for part in range(KV_ROWS // BLOCK):
            attend(pl.multiple_of(r0 + part * BLOCK, BLOCK), part)
        return carry

    lax.fori_loop(0, KV_CHUNKS // 2, kv_step, 0)
    pl.semaphore_wait(barrier, PEERS - 1 + TP - 1)
    aux_sent = [None] * PEERS
    for k in range(1, PEERS):
        aux_sent[k] = send(aux_send.at[k], aux_recv.at[k], s_aux.at[k], r_aux.at[k], to_ad(OFFSETS[k], 1))
    aux_recv[0] = aux_send[0]
    opposite(0)
    lax.fori_loop(KV_CHUNKS // 2, KV_CHUNKS, kv_step, 0)

    packed[...] = mm(sel[...], att[...]).astype(BF).reshape(PEERS, CAP, WIDTH)
    fwd = [None] * PEERS
    for k in range(1, PEERS):
        fwd[k] = send(packed.at[k], arrived.at[k], s_fwd.at[k], r_fwd.at[k], to_ad(OFFSETS[k], 1))
    weights[1].start()
    shrink_copy.start()
    arrived[0] = packed[0]

    opposite(1)
    weights[2].start()
    expand_copy.start()
    weights[3].start()
    part(1, half, 2 * half, to_send(0, 1, HALF))
    part(1, 0, half, to_hold(0, 0))
    shrink_copy.wait()
    expand_copy.wait()

    spread_mask = (iota((AUX, HELD * RANK), 0) == iota((AUX, HELD * RANK), 1) // RANK).astype(F32).astype(BF)
    low = iota((QROWS // 2, 2 * RANK), 1) < RANK
    ar = [None] * QUARTERS
    back = [None] * PEERS

    def down(g):
        for k in range(g * QPEERS, (g + 1) * QPEERS):
            if k:
                aux_sent[k].wait_recv()
                fwd[k].wait_recv()
        rows = arrived[g * QPEERS : (g + 1) * QPEERS].reshape(QROWS, WIDTH)
        full = mm(rows, shrink[...])
        pick = mm(aux_recv[g * QPEERS : (g + 1) * QPEERS].reshape(QROWS, AUX), spread_mask)
        picks[g] = pick.astype(BF)
        kept = jnp.where(pick > 0.5, full, 0.0)
        folded = sum(kept[:, i * 128 : (i + 1) * 128] for i in range(HELD * RANK // 128))
        both = folded + pltpu.roll(folded, RANK, 1)
        half_rows = jnp.where(low, both[: QROWS // 2], both[QROWS // 2 :])
        ar_own[g] = half_rows
        ar_send[g] = half_rows.astype(BF)
        ar[g] = [
            send(ar_send.at[g], ar_recv.at[g, d], s_ar.at[g, d], r_ar.at[g, d], to_tp(d + 1))
            for d in range(TP - 1)
        ]

    def up(g):
        for copy in ar[g]:
            copy.wait()
        total = ar_own[g]
        for d in range(TP - 1):
            total = total + ar_recv[g, d].astype(F32)
        other = pltpu.roll(total, RANK, 1)
        both = jnp.concatenate([jnp.where(low, total, other), jnp.where(low, other, total)], axis=0).astype(BF)
        spread = jnp.concatenate([both] * (HELD * RANK // 128), axis=1) * picks[g]
        peers = slice(g * QPEERS, (g + 1) * QPEERS)
        for j in range(CHUNK // tile):
            columns = slice(j * tile, (j + 1) * tile)
            wid[peers, :, columns] = mm(spread, expand[:, columns]).astype(BF).reshape(QPEERS, CAP, tile)
        for k in range(g * QPEERS, (g + 1) * QPEERS):
            if k:
                back[k] = send(wid.at[k], ret.at[k], s_back.at[k], r_back.at[k], to_ad(OFFSETS[k], -1))
            else:
                ret[0] = wid[0]

    down(0)
    part(2, 0, half, to_send(1, 1, 0))
    part(2, half, 2 * half, to_hold(1, HALF))
    down(1)
    part(3, 0, 2 * half, to_own)
    down(2)
    sent[0][1] = ring(0, 1)
    sent[1][1] = ring(1, 1)
    up(0)
    down(3)
    for d in range(2):
        sent_half[d].wait_recv()
        sent[d][0].wait_recv()
        rs_send[d, 2] = (hold[d] + rs_recv[d, 0].astype(F32)).astype(BF)
        sent[d][2] = ring(d, 2)
    up(1)
    up(2)
    up(3)

    for d in range(2):
        sent[d][1].wait_recv()
    own[:, :HALF] += rs_recv[1, 1].astype(F32)
    own[:, HALF:] += rs_recv[0, 1].astype(F32)

    def returned(g, last=False):
        for k in range(g * QPEERS, (g + 1) * QPEERS):
            if k:
                back[k].wait_recv()
        chosen = sel_t[:, g * QROWS : (g + 1) * QROWS]
        for j in range(CHUNK // tile):
            columns = slice(j * tile, (j + 1) * tile)
            values = ret[g * QPEERS : (g + 1) * QPEERS, :, columns].reshape(QROWS, tile)
            value = own[:, columns] + mm(chosen, values)
            if last:
                out_ref[:, columns] = value.astype(BF)
            else:
                own[:, columns] = value

    returned(0)
    returned(1)
    for d in range(2):
        sent[d][2].wait_recv()
    own[:, :HALF] += rs_recv[0, 2].astype(F32)
    own[:, HALF:] += rs_recv[1, 2].astype(F32)
    returned(2)
    returned(3, last=True)

    for k in range(1, PEERS):
        aux_sent[k].wait_send()
        fwd[k].wait_send()
        back[k].wait_send()
    for d in range(2):
        sent_half[d].wait_send()
        for stage in range(3):
            sent[d][stage].wait_send()


def shards(
    queries,
    key_cache,
    value_cache,
    new_key,
    new_value,
    lengths,
    out_weight,
    shrink_weight,
    expand_weight,
    adapter_id,
    adapter_slot,
):
    dma = pltpu.SemaphoreType.DMA
    hbm = pl.BlockSpec(memory_space=pl.ANY)
    vmem = pl.BlockSpec(memory_space=pltpu.VMEM)
    return pl.pallas_call(
        kernel,
        out_shape=pltpu.VMEM((ROWS, CHUNK), BF),
        in_specs=[hbm] * 11,
        out_specs=vmem,
        scratch_shapes=[
            pltpu.SMEM((ROWS,), jnp.int32),
            pltpu.VMEM((1, ROWS), jnp.int32),
            pltpu.VMEM((1, ROWS), jnp.int32),
            pltpu.VMEM((ROWS, WIDTH), BF),
            pltpu.VMEM((ROWS, SLOTS, DIM), BF),
            pltpu.VMEM((ROWS, SLOTS, DIM), BF),
            pltpu.VMEM((ROWS, DIM), BF),
            pltpu.VMEM((ROWS, DIM), BF),
            pltpu.VMEM((TP, WIDTH, CHUNK), BF),
            pltpu.VMEM((WIDTH, HELD * RANK), BF),
            pltpu.VMEM((HELD * RANK, CHUNK), BF),
            pltpu.VMEM((KV_ROWS // BLOCK, BLOCK * HEADS, DIM), F32),
            pltpu.VMEM((KV_ROWS // BLOCK, BLOCK * HEADS, DIM), F32),
            pltpu.VMEM((ROWS, WIDTH), BF),
            pltpu.VMEM((PEERS * CAP, ROWS), BF),
            pltpu.VMEM((ROWS, PEERS * CAP), BF),
            pltpu.VMEM((PEERS, CAP, WIDTH), BF),
            pltpu.VMEM((PEERS, CAP, WIDTH), BF),
            pltpu.VMEM((PEERS, CAP, AUX), BF),
            pltpu.VMEM((PEERS, CAP, AUX), BF),
            pltpu.VMEM((PEERS, CAP, CHUNK), BF),
            pltpu.VMEM((PEERS, CAP, CHUNK), BF),
            pltpu.VMEM((QUARTERS, QROWS, HELD * RANK), BF),
            pltpu.VMEM((QUARTERS, QROWS // 2, 2 * RANK), F32),
            pltpu.VMEM((QUARTERS, QROWS // 2, 2 * RANK), BF),
            pltpu.VMEM((QUARTERS, TP - 1, QROWS // 2, 2 * RANK), BF),
            pltpu.VMEM((2, 3, ROWS, HALF), BF),
            pltpu.VMEM((2, 3, ROWS, HALF), BF),
            pltpu.VMEM((2, ROWS, HALF), F32),
            pltpu.VMEM((ROWS, CHUNK), F32),
            dma((8,)),
            dma((KV_CHUNKS,)),
            dma((KV_CHUNKS,)),
            dma((TP,)),
            dma((PEERS,)),
            dma((PEERS,)),
            dma((PEERS,)),
            dma((PEERS,)),
            dma((QUARTERS, TP - 1)),
            dma((QUARTERS, TP - 1)),
            dma((2, 4)),
            dma((2, 4)),
            dma((PEERS,)),
            dma((PEERS,)),
        ],
        compiler_params=pltpu.CompilerParams(
            collective_id=0, has_side_effects=True, vmem_limit_bytes=58 * 2**20
        ),
    )(
        queries,
        key_cache,
        value_cache,
        new_key,
        new_value,
        out_weight,
        shrink_weight,
        expand_weight,
        lengths,
        adapter_id.reshape(1, ROWS),
        adapter_slot.reshape(1, ROWS),
    )


def solution(mesh):
    in_specs = (
        P("ad", "tp"),
        P("ad", None, "tp"),
        P("ad", None, "tp"),
        P("ad", "tp"),
        P("ad", "tp"),
        P("ad"),
        P("tp", None),
        P("tp", "ad"),
        P("ad", "tp"),
        P("ad"),
        P(),
    )
    out_specs = P("ad", "tp")
    return jax.shard_map(shards, mesh=mesh, in_specs=in_specs, out_specs=out_specs, check_vma=False)
```

```python
import math

import jax
import jax.numpy as jnp
from jax import lax
from jax.experimental import pallas as pl
from jax.experimental.pallas import tpu as pltpu
from jax.sharding import PartitionSpec as P

HEADS = 8
DIM = 128
RANK = 64
HELD = 8
ROWS = 256
SLOTS = 128
TP = 4
PEERS = 32
CAP = 16
WIDTH = HEADS * DIM
CHUNK = 2048
HALF = CHUNK // 2
AUX = 128
QUARTERS = 4
QPEERS = PEERS // QUARTERS
QROWS = QPEERS * CAP
KV_CHUNKS = 8
KV_ROWS = ROWS // KV_CHUNKS
KV_AHEAD = 2
W_AFTER = 1
BLOCK = 16
BF = jnp.bfloat16
F32 = jnp.float32
MESH = pl.DeviceIdType.MESH
NT = (((1,), (1,)), ((), ()))


def peer_offsets():
    quarters = [[] for _ in range(QUARTERS)]
    for dx in range(4):
        for dz in range(4):
            for dc in range(2):
                quarters[(dx + dz) % 2 + 2 * dc].append((dx, dz, dc))
    return [offset for quarter in quarters for offset in quarter]


OFFSETS = peer_offsets()
ORDER = (5, 2, 6, 1, 7, 3, 4, 0)


def iota(shape, axis):
    return lax.broadcasted_iota(jnp.int32, shape, axis)


def mm(a, b):
    return jnp.dot(a, b, preferred_element_type=F32)


def mm_nt(a, b):
    return lax.dot_general(a, b, NT, preferred_element_type=F32)


def kernel(
    q_hbm, k_hbm, v_hbm, nk_hbm, nv_hbm, w_hbm, shrink_hbm, expand_hbm, len_hbm, id_hbm, slot_hbm,
    out_ref,
    len_ref, id_ref, slot_ref,
    q, kbuf, vbuf, nk, nv, wbuf, shrink, expand, qscr, oscr, att, sel, sel_t,
    packed, arrived, aux_send, aux_recv, wid, ret, picks, ar_own, ar_send, ar_recv, rs_send, rs_recv, hold, own,
    sem_small, sem_k, sem_v, sem_w,
    s_fwd, r_fwd, s_back, r_back, s_ar, r_ar, s_rs, r_rs, s_aux, r_aux,
):
    me_t = lax.axis_index("tp")
    me_a = lax.axis_index("ad")
    me_x, me_z, me_c = me_a // 8, (me_a // 2) % 4, me_a % 2

    def ad_of(offset, sign):
        dx, dz, dc = offset
        x = (me_x + (sign * dx) % 4) % 4
        z = (me_z + (sign * dz) % 4) % 4
        return (x * 4 + z) * 2 + (me_c + dc) % 2

    def to_ad(offset, sign):
        return (me_t, ad_of(offset, sign))

    def to_tp(step):
        return ((me_t + step) % TP, me_a)

    def fetch(src, dst, sem):
        copy = pltpu.make_async_copy(src, dst, sem)
        copy.start()
        return copy

    named_copies = [fetch(id_hbm, id_ref, sem_small.at[5]), fetch(slot_hbm, slot_ref, sem_small.at[6])]
    small = [
        fetch(len_hbm, len_ref, sem_small.at[7]),
        fetch(q_hbm, q, sem_small.at[0]),
        fetch(nk_hbm, nk, sem_small.at[1]),
        fetch(nv_hbm, nv, sem_small.at[2]),
    ]

    def kv_copies(i):
        rows = pl.ds(pl.multiple_of(i * KV_ROWS, KV_ROWS), KV_ROWS)
        return (
            pltpu.make_async_copy(k_hbm.at[rows], kbuf.at[rows], sem_k.at[i]),
            pltpu.make_async_copy(v_hbm.at[rows], vbuf.at[rows], sem_v.at[i]),
        )

    def start_kv(i):
        for copy in kv_copies(i):
            copy.start()

    for i in range(KV_AHEAD):
        start_kv(i)

    def weight_copy(i):
        column = pl.multiple_of(((me_t + (2, 1, 3, 0)[i]) % TP) * CHUNK, CHUNK)
        return pltpu.make_async_copy(w_hbm.at[:, pl.ds(column, CHUNK)], wbuf.at[i], sem_w.at[i])

    weights = [weight_copy(i) for i in range(TP)]
    shrink_copy = pltpu.make_async_copy(shrink_hbm, shrink, sem_small.at[3])
    expand_copy = pltpu.make_async_copy(expand_hbm, expand, sem_small.at[4])

    barrier = pltpu.get_barrier_semaphore()
    for offset in OFFSETS[1:]:
        pl.semaphore_signal(barrier, inc=1, device_id=to_ad(offset, 1), device_id_type=MESH)
    for step in (1, 2, 3):
        pl.semaphore_signal(barrier, inc=1, device_id=to_tp(step), device_id_type=MESH)

    for copy in named_copies:
        copy.wait()
    named = (iota((ROWS, ROWS), 0) == id_ref[...]).astype(F32).astype(BF)
    catalog = jnp.broadcast_to(slot_ref[...].astype(F32), (8, ROWS)).astype(BF)
    slot = mm(catalog, named)[0:1, :].astype(jnp.int32)
    owner = lax.shift_right_logical(slot, 3)
    local = jnp.bitwise_and(slot, HELD - 1)
    dx = jnp.bitwise_and(lax.shift_right_logical(owner, 3) - me_x, 3)
    dz = jnp.bitwise_and(lax.shift_right_logical(owner, 1) - me_z, 3)
    dc = jnp.bitwise_and(owner - me_c, 1)
    peer = jnp.bitwise_and(dx + dz, 1) * 8 + dc * 16 + dx * 2 + lax.shift_right_logical(dz, 1)
    hits = (iota((PEERS, ROWS), 0) == peer).astype(F32)
    before = (iota((ROWS, ROWS), 0) < iota((ROWS, ROWS), 1)).astype(F32).astype(BF)
    earlier = mm(hits.astype(BF), before)
    rank = jnp.sum(hits * earlier, axis=0, keepdims=True).astype(jnp.int32)
    place = peer * CAP + rank
    sel[...] = (iota((PEERS * CAP, ROWS), 0) == place).astype(F32).astype(BF)
    eye = (iota((ROWS, ROWS), 0) == iota((ROWS, ROWS), 1)).astype(F32).astype(BF)
    sel_t[...] = mm_nt(eye, sel[...]).astype(BF)
    local_hot = (iota((AUX, ROWS), 0) == local).astype(F32).astype(BF)
    aux = mm_nt(sel[...], local_hot).astype(BF)
    aux_send[...] = aux.reshape(PEERS, CAP, AUX)

    for copy in small:
        copy.wait()
    scale = 1.0 / math.sqrt(DIM)
    group_rows = BLOCK * HEADS
    own_mask = iota((group_rows, BLOCK), 1) == iota((group_rows, BLOCK), 0) // HEADS
    lane = iota((HEADS, SLOTS), 1)
    blank = jnp.zeros((HEADS, DIM), F32)

    def attend(r0, part):
        rows = pl.ds(r0, BLOCK)
        qb = q[rows, :].astype(F32)
        for h in range(HEADS):
            qscr[part, pl.ds(h, BLOCK, stride=HEADS), :] = qb[:, h * DIM : (h + 1) * DIM]
        qv = qscr[part].astype(BF)
        fresh = mm_nt(qv, nk[rows, :]) * scale
        fresh = jnp.sum(jnp.where(own_mask, fresh, 0.0), axis=1, keepdims=True)
        pieces = []
        for i in range(BLOCK // 2):
            keys = kbuf[pl.ds(r0 + 2 * i, 2)].reshape(2 * SLOTS, DIM)
            s = mm_nt(qv[16 * i : 16 * i + 16], keys)
            for j in range(2):
                piece = s[8 * j : 8 * j + 8, SLOTS * j : SLOTS * (j + 1)] * scale
                pieces.append(jnp.where(lane < len_ref[r0 + 2 * i + j], piece, -jnp.inf))
        scores = jnp.concatenate(pieces, axis=0)
        top = jnp.maximum(jnp.max(scores, axis=1, keepdims=True), fresh)
        expo = jnp.exp(scores - top)
        fresh_expo = jnp.exp(fresh - top)
        total = jnp.sum(expo, axis=1, keepdims=True) + fresh_expo
        probs = expo / total
        fresh_prob = jnp.where(own_mask, fresh_expo / total, 0.0).astype(BF)
        mixed = []
        for i in range(BLOCK // 2):
            values = vbuf[pl.ds(r0 + 2 * i, 2)].reshape(2 * SLOTS, DIM)
            first = jnp.concatenate([probs[16 * i : 16 * i + 8], blank], axis=1)
            second = jnp.concatenate([blank, probs[16 * i + 8 : 16 * i + 16]], axis=1)
            mixed.append(mm(jnp.concatenate([first, second], axis=0).astype(BF), values))
        oscr[part] = jnp.concatenate(mixed, axis=0) + mm(fresh_prob, nv[rows, :])
        for h in range(HEADS):
            att[rows, h * DIM : (h + 1) * DIM] = oscr[part, pl.ds(h, BLOCK, stride=HEADS), :].astype(BF)

    def send(src, dst, s, r, device):
        copy = pltpu.make_async_remote_copy(
            src_ref=src, dst_ref=dst, send_sem=s, recv_sem=r, device_id=device, device_id_type=MESH
        )
        copy.start()
        return copy

    tile = 512

    def ring(d, stage):
        return send(
            rs_send.at[d, stage], rs_recv.at[d, stage], s_rs.at[d, stage], r_rs.at[d, stage],
            to_tp(1 if d == 0 else 3),
        )

    def to_send(d, stage, start):
        def store(column, value):
            rs_send[d, stage, :, pl.ds(pl.multiple_of(column - start, tile), tile)] = value.astype(BF)

        return store

    def to_hold(d, start):
        def store(column, value):
            hold[d, :, pl.ds(pl.multiple_of(column - start, tile), tile)] = value

        return store

    def to_own(column, value):
        own[:, pl.ds(column, tile)] = value

    half = HALF // tile
    weights_done = [False] * TP

    def part(i, first, last, store):
        if not weights_done[i]:
            weights[i].wait()
            weights_done[i] = True

        def step(j, carry):
            column = pl.multiple_of(j * tile, tile)
            store(column, mm(att[...], wbuf[i, :, pl.ds(column, tile)]))
            return carry

        lax.fori_loop(first, last, step, 0)

    sent = [[None] * 3 for _ in range(2)]
    sent_half = [None, None]

    def ring_half(d, part_of):
        rows = pl.ds(part_of * (ROWS // 2), ROWS // 2)
        slot_of = 0 if part_of else 3
        return send(
            rs_send.at[d, 0, rows], rs_recv.at[d, 0, rows], s_rs.at[d, slot_of], r_rs.at[d, slot_of],
            to_tp(1 if d == 0 else 3),
        )

    def opposite(part_of):
        if part_of == 0:
            weights[0].wait()
        rows = slice(part_of * (ROWS // 2), (part_of + 1) * (ROWS // 2))
        for d in range(2):
            for j in range(half):
                columns = slice(j * tile, (j + 1) * tile)
                value = mm(att[rows, :], wbuf[0, :, d * HALF + j * tile : d * HALF + (j + 1) * tile])
                rs_send[d, 0, rows, columns] = value.astype(BF)
            copy = ring_half(d, part_of)
            if part_of:
                sent[d][0] = copy
            else:
                sent_half[d] = copy

    def kv_step(i, carry):
        for copy in kv_copies(i):
            copy.wait()

        @pl.when(i < KV_CHUNKS - KV_AHEAD)
        def _():
            start_kv(i + KV_AHEAD)

        @pl.when(i == W_AFTER)
        def _():
            weights[0].start()

        @pl.when(i == KV_CHUNKS - KV_AHEAD)
        def _():
            shrink_copy.start()

        r0 = pl.multiple_of(i * KV_ROWS, KV_ROWS)
        for part in range(KV_ROWS // BLOCK):
            attend(pl.multiple_of(r0 + part * BLOCK, BLOCK), part)
        return carry

    lax.fori_loop(0, KV_CHUNKS // 2, kv_step, 0)
    pl.semaphore_wait(barrier, PEERS - 1 + TP - 1)
    aux_sent = [None] * PEERS
    for k in range(1, PEERS):
        aux_sent[k] = send(aux_send.at[k], aux_recv.at[k], s_aux.at[k], r_aux.at[k], to_ad(OFFSETS[k], 1))
    aux_recv[0] = aux_send[0]
    opposite(0)
    lax.fori_loop(KV_CHUNKS // 2, KV_CHUNKS, kv_step, 0)

    packed[...] = mm(sel[...], att[...]).astype(BF).reshape(PEERS, CAP, WIDTH)
    fwd = [None] * PEERS
    for k in [q * QPEERS + j for q in range(QUARTERS) for j in ORDER][:PEERS]:
        if k == 0:
            continue
        fwd[k] = send(packed.at[k], arrived.at[k], s_fwd.at[k], r_fwd.at[k], to_ad(OFFSETS[k], 1))
    weights[1].start()
    arrived[0] = packed[0]

    opposite(1)
    weights[2].start()
    expand_copy.start()
    weights[3].start()
    part(1, half, 2 * half, to_send(0, 1, HALF))
    part(1, 0, half, to_hold(0, 0))
    shrink_copy.wait()
    expand_copy.wait()

    spread_mask = (iota((AUX, HELD * RANK), 0) == iota((AUX, HELD * RANK), 1) // RANK).astype(F32).astype(BF)
    low = iota((QROWS // 2, 2 * RANK), 1) < RANK
    ar = [None] * QUARTERS
    back = [None] * PEERS

    def down(g):
        for k in range(g * QPEERS, (g + 1) * QPEERS):
            if k:
                aux_sent[k].wait_recv()
                fwd[k].wait_recv()
        rows = arrived[g * QPEERS : (g + 1) * QPEERS].reshape(QROWS, WIDTH)
        full = mm(rows, shrink[...])
        pick = mm(aux_recv[g * QPEERS : (g + 1) * QPEERS].reshape(QROWS, AUX), spread_mask)
        picks[g] = pick.astype(BF)
        kept = jnp.where(pick > 0.5, full, 0.0)
        folded = sum(kept[:, i * 128 : (i + 1) * 128] for i in range(HELD * RANK // 128))
        both = folded + pltpu.roll(folded, RANK, 1)
        half_rows = jnp.where(low, both[: QROWS // 2], both[QROWS // 2 :])
        ar_own[g] = half_rows
        ar_send[g] = half_rows.astype(BF)
        ar[g] = [
            send(ar_send.at[g], ar_recv.at[g, d], s_ar.at[g, d], r_ar.at[g, d], to_tp(d + 1))
            for d in range(TP - 1)
        ]

    def up(g):
        for copy in ar[g]:
            copy.wait()
        total = ar_own[g]
        for d in range(TP - 1):
            total = total + ar_recv[g, d].astype(F32)
        other = pltpu.roll(total, RANK, 1)
        both = jnp.concatenate([jnp.where(low, total, other), jnp.where(low, other, total)], axis=0).astype(BF)
        spread = jnp.concatenate([both] * (HELD * RANK // 128), axis=1) * picks[g]
        peers = slice(g * QPEERS, (g + 1) * QPEERS)
        for j in range(CHUNK // tile):
            columns = slice(j * tile, (j + 1) * tile)
            wid[peers, :, columns] = mm(spread, expand[:, columns]).astype(BF).reshape(QPEERS, CAP, tile)
        for k in range(g * QPEERS, (g + 1) * QPEERS):
            if k:
                back[k] = send(wid.at[k], ret.at[k], s_back.at[k], r_back.at[k], to_ad(OFFSETS[k], -1))
            else:
                ret[0] = wid[0]

    down(0)
    part(2, 0, half, to_send(1, 1, 0))
    part(2, half, 2 * half, to_hold(1, HALF))
    down(1)
    sent[0][1] = ring(0, 1)
    sent[1][1] = ring(1, 1)
    part(3, 0, 2 * half, to_own)
    down(2)
    up(0)
    up(1)
    down(3)
    for d in range(2):
        sent_half[d].wait_recv()
        sent[d][0].wait_recv()
        rs_send[d, 2] = (hold[d] + rs_recv[d, 0].astype(F32)).astype(BF)
        sent[d][2] = ring(d, 2)
    up(2)
    up(3)

    for d in range(2):
        sent[d][1].wait_recv()
    own[:, :HALF] += rs_recv[1, 1].astype(F32)
    own[:, HALF:] += rs_recv[0, 1].astype(F32)

    def returned(g, last=False):
        for k in range(g * QPEERS, (g + 1) * QPEERS):
            if k:
                back[k].wait_recv()
        chosen = sel_t[:, g * QROWS : (g + 1) * QROWS]
        for j in range(CHUNK // tile):
            columns = slice(j * tile, (j + 1) * tile)
            values = ret[g * QPEERS : (g + 1) * QPEERS, :, columns].reshape(QROWS, tile)
            value = own[:, columns] + mm(chosen, values)
            if last:
                out_ref[:, columns] = value.astype(BF)
            else:
                own[:, columns] = value

    returned(0)
    returned(1)
    for d in range(2):
        sent[d][2].wait_recv()
    own[:, :HALF] += rs_recv[0, 2].astype(F32)
    own[:, HALF:] += rs_recv[1, 2].astype(F32)
    returned(2)
    returned(3, last=True)

    for k in range(1, PEERS):
        aux_sent[k].wait_send()
        fwd[k].wait_send()
        back[k].wait_send()
    for d in range(2):
        sent_half[d].wait_send()
        for stage in range(3):
            sent[d][stage].wait_send()


def shards(
    queries,
    key_cache,
    value_cache,
    new_key,
    new_value,
    lengths,
    out_weight,
    shrink_weight,
    expand_weight,
    adapter_id,
    adapter_slot,
):
    dma = pltpu.SemaphoreType.DMA
    hbm = pl.BlockSpec(memory_space=pl.ANY)
    vmem = pl.BlockSpec(memory_space=pltpu.VMEM)
    return pl.pallas_call(
        kernel,
        out_shape=pltpu.VMEM((ROWS, CHUNK), BF),
        in_specs=[hbm] * 11,
        out_specs=vmem,
        scratch_shapes=[
            pltpu.SMEM((ROWS,), jnp.int32),
            pltpu.VMEM((1, ROWS), jnp.int32),
            pltpu.VMEM((1, ROWS), jnp.int32),
            pltpu.VMEM((ROWS, WIDTH), BF),
            pltpu.VMEM((ROWS, SLOTS, DIM), BF),
            pltpu.VMEM((ROWS, SLOTS, DIM), BF),
            pltpu.VMEM((ROWS, DIM), BF),
            pltpu.VMEM((ROWS, DIM), BF),
            pltpu.VMEM((TP, WIDTH, CHUNK), BF),
            pltpu.VMEM((WIDTH, HELD * RANK), BF),
            pltpu.VMEM((HELD * RANK, CHUNK), BF),
            pltpu.VMEM((KV_ROWS // BLOCK, BLOCK * HEADS, DIM), F32),
            pltpu.VMEM((KV_ROWS // BLOCK, BLOCK * HEADS, DIM), F32),
            pltpu.VMEM((ROWS, WIDTH), BF),
            pltpu.VMEM((PEERS * CAP, ROWS), BF),
            pltpu.VMEM((ROWS, PEERS * CAP), BF),
            pltpu.VMEM((PEERS, CAP, WIDTH), BF),
            pltpu.VMEM((PEERS, CAP, WIDTH), BF),
            pltpu.VMEM((PEERS, CAP, AUX), BF),
            pltpu.VMEM((PEERS, CAP, AUX), BF),
            pltpu.VMEM((PEERS, CAP, CHUNK), BF),
            pltpu.VMEM((PEERS, CAP, CHUNK), BF),
            pltpu.VMEM((QUARTERS, QROWS, HELD * RANK), BF),
            pltpu.VMEM((QUARTERS, QROWS // 2, 2 * RANK), F32),
            pltpu.VMEM((QUARTERS, QROWS // 2, 2 * RANK), BF),
            pltpu.VMEM((QUARTERS, TP - 1, QROWS // 2, 2 * RANK), BF),
            pltpu.VMEM((2, 3, ROWS, HALF), BF),
            pltpu.VMEM((2, 3, ROWS, HALF), BF),
            pltpu.VMEM((2, ROWS, HALF), F32),
            pltpu.VMEM((ROWS, CHUNK), F32),
            dma((8,)),
            dma((KV_CHUNKS,)),
            dma((KV_CHUNKS,)),
            dma((TP,)),
            dma((PEERS,)),
            dma((PEERS,)),
            dma((PEERS,)),
            dma((PEERS,)),
            dma((QUARTERS, TP - 1)),
            dma((QUARTERS, TP - 1)),
            dma((2, 4)),
            dma((2, 4)),
            dma((PEERS,)),
            dma((PEERS,)),
        ],
        compiler_params=pltpu.CompilerParams(
            collective_id=0, has_side_effects=True, vmem_limit_bytes=58 * 2**20
        ),
    )(
        queries,
        key_cache,
        value_cache,
        new_key,
        new_value,
        out_weight,
        shrink_weight,
        expand_weight,
        lengths,
        adapter_id.reshape(1, ROWS),
        adapter_slot.reshape(1, ROWS),
    )


def solution(mesh):
    in_specs = (
        P("ad", "tp"),
        P("ad", None, "tp"),
        P("ad", None, "tp"),
        P("ad", "tp"),
        P("ad", "tp"),
        P("ad"),
        P("tp", None),
        P("tp", "ad"),
        P("ad", "tp"),
        P("ad"),
        P(),
    )
    out_specs = P("ad", "tp")
    return jax.shard_map(shards, mesh=mesh, in_specs=in_specs, out_specs=out_specs, check_vma=False)
```

```python
import math

import jax
import jax.numpy as jnp
from jax import lax
from jax.experimental import pallas as pl
from jax.experimental.pallas import tpu as pltpu
from jax.sharding import PartitionSpec as P

HEADS = 8
DIM = 128
RANK = 64
HELD = 8
ROWS = 256
SLOTS = 128
TP = 4
PEERS = 32
CAP = 16
WIDTH = HEADS * DIM
CHUNK = 2048
HALF = CHUNK // 2
AUX = 128
PACK = WIDTH + AUX
QUARTERS = 4
QPEERS = PEERS // QUARTERS
QROWS = QPEERS * CAP
KV_CHUNKS = 8
KV_ROWS = ROWS // KV_CHUNKS
KV_AHEAD = 2
W_AFTER = 1
BLOCK = 16
BF = jnp.bfloat16
F32 = jnp.float32
MESH = pl.DeviceIdType.MESH
NT = (((1,), (1,)), ((), ()))


def peer_offsets():
    quarters = [[] for _ in range(QUARTERS)]
    for dx in range(4):
        for dz in range(4):
            for dc in range(2):
                quarters[(dx + dz) % 2 + 2 * dc].append((dx, dz, dc))
    return [offset for quarter in quarters for offset in quarter]


OFFSETS = peer_offsets()
ORDER = (5, 2, 6, 1, 7, 3, 4, 0)


def iota(shape, axis):
    return lax.broadcasted_iota(jnp.int32, shape, axis)


def mm(a, b):
    return jnp.dot(a, b, preferred_element_type=F32)


def mm_nt(a, b):
    return lax.dot_general(a, b, NT, preferred_element_type=F32)


def kernel(
    q_hbm, k_hbm, v_hbm, nk_hbm, nv_hbm, w_hbm, shrink_hbm, expand_hbm, len_hbm, id_hbm, slot_hbm,
    out_ref,
    len_ref, id_ref, slot_ref,
    q, kbuf, vbuf, nk, nv, wbuf, shrink, expand, qscr, oscr, att, sel, sel_t,
    packed, arrived, wid, ret, picks, ar_own, ar_send, ar_recv, rs_send, rs_recv, hold, own,
    sem_small, sem_k, sem_v, sem_w,
    s_fwd, r_fwd, s_back, r_back, s_ar, r_ar, s_rs, r_rs,
):
    me_t = lax.axis_index("tp")
    me_a = lax.axis_index("ad")
    me_x, me_z, me_c = me_a // 8, (me_a // 2) % 4, me_a % 2

    def ad_of(offset, sign):
        dx, dz, dc = offset
        x = (me_x + (sign * dx) % 4) % 4
        z = (me_z + (sign * dz) % 4) % 4
        return (x * 4 + z) * 2 + (me_c + dc) % 2

    def to_ad(offset, sign):
        return (me_t, ad_of(offset, sign))

    def to_tp(step):
        return ((me_t + step) % TP, me_a)

    def fetch(src, dst, sem):
        copy = pltpu.make_async_copy(src, dst, sem)
        copy.start()
        return copy

    named_copies = [fetch(id_hbm, id_ref, sem_small.at[5]), fetch(slot_hbm, slot_ref, sem_small.at[6])]
    small = [
        fetch(len_hbm, len_ref, sem_small.at[7]),
        fetch(q_hbm, q, sem_small.at[0]),
        fetch(nk_hbm, nk, sem_small.at[1]),
        fetch(nv_hbm, nv, sem_small.at[2]),
    ]

    def kv_copies(i):
        rows = pl.ds(pl.multiple_of(i * KV_ROWS, KV_ROWS), KV_ROWS)
        return (
            pltpu.make_async_copy(k_hbm.at[rows], kbuf.at[rows], sem_k.at[i]),
            pltpu.make_async_copy(v_hbm.at[rows], vbuf.at[rows], sem_v.at[i]),
        )

    def start_kv(i):
        for copy in kv_copies(i):
            copy.start()

    for i in range(KV_AHEAD):
        start_kv(i)

    def weight_copy(i):
        column = pl.multiple_of(((me_t + (2, 1, 3, 0)[i]) % TP) * CHUNK, CHUNK)
        return pltpu.make_async_copy(w_hbm.at[:, pl.ds(column, CHUNK)], wbuf.at[i], sem_w.at[i])

    weights = [weight_copy(i) for i in range(TP)]
    shrink_copy = pltpu.make_async_copy(shrink_hbm, shrink, sem_small.at[3])
    expand_copy = pltpu.make_async_copy(expand_hbm, expand, sem_small.at[4])

    barrier = pltpu.get_barrier_semaphore()
    for offset in OFFSETS[1:]:
        pl.semaphore_signal(barrier, inc=1, device_id=to_ad(offset, 1), device_id_type=MESH)
    for step in (1, 2, 3):
        pl.semaphore_signal(barrier, inc=1, device_id=to_tp(step), device_id_type=MESH)

    for copy in named_copies:
        copy.wait()
    named = (iota((ROWS, ROWS), 0) == id_ref[...]).astype(F32).astype(BF)
    catalog = jnp.broadcast_to(slot_ref[...].astype(F32), (8, ROWS)).astype(BF)
    slot = mm(catalog, named)[0:1, :].astype(jnp.int32)
    owner = lax.shift_right_logical(slot, 3)
    local = jnp.bitwise_and(slot, HELD - 1)
    dx = jnp.bitwise_and(lax.shift_right_logical(owner, 3) - me_x, 3)
    dz = jnp.bitwise_and(lax.shift_right_logical(owner, 1) - me_z, 3)
    dc = jnp.bitwise_and(owner - me_c, 1)
    peer = jnp.bitwise_and(dx + dz, 1) * 8 + dc * 16 + dx * 2 + lax.shift_right_logical(dz, 1)
    hits = (iota((PEERS, ROWS), 0) == peer).astype(F32)
    before = (iota((ROWS, ROWS), 0) < iota((ROWS, ROWS), 1)).astype(F32).astype(BF)
    earlier = mm(hits.astype(BF), before)
    rank = jnp.sum(hits * earlier, axis=0, keepdims=True).astype(jnp.int32)
    place = peer * CAP + rank
    sel[...] = (iota((PEERS * CAP, ROWS), 0) == place).astype(F32).astype(BF)
    eye = (iota((ROWS, ROWS), 0) == iota((ROWS, ROWS), 1)).astype(F32).astype(BF)
    sel_t[...] = mm_nt(eye, sel[...]).astype(BF)
    local_hot = (iota((AUX, ROWS), 0) == local).astype(F32).astype(BF)
    aux = mm_nt(sel[...], local_hot).astype(BF)
    packed[:, :, WIDTH:] = aux.reshape(PEERS, CAP, AUX)

    for copy in small:
        copy.wait()
    scale = 1.0 / math.sqrt(DIM)
    group_rows = BLOCK * HEADS
    own_mask = iota((group_rows, BLOCK), 1) == iota((group_rows, BLOCK), 0) // HEADS
    lane = iota((HEADS, SLOTS), 1)
    blank = jnp.zeros((HEADS, DIM), F32)

    def attend(r0, part):
        rows = pl.ds(r0, BLOCK)
        qb = q[rows, :].astype(F32)
        for h in range(HEADS):
            qscr[part, pl.ds(h, BLOCK, stride=HEADS), :] = qb[:, h * DIM : (h + 1) * DIM]
        qv = qscr[part].astype(BF)
        fresh = mm_nt(qv, nk[rows, :]) * scale
        fresh = jnp.sum(jnp.where(own_mask, fresh, 0.0), axis=1, keepdims=True)
        pieces = []
        for i in range(BLOCK // 2):
            keys = kbuf[pl.ds(r0 + 2 * i, 2)].reshape(2 * SLOTS, DIM)
            s = mm_nt(qv[16 * i : 16 * i + 16], keys)
            for j in range(2):
                piece = s[8 * j : 8 * j + 8, SLOTS * j : SLOTS * (j + 1)] * scale
                pieces.append(jnp.where(lane < len_ref[r0 + 2 * i + j], piece, -jnp.inf))
        scores = jnp.concatenate(pieces, axis=0)
        top = jnp.maximum(jnp.max(scores, axis=1, keepdims=True), fresh)
        expo = jnp.exp(scores - top)
        fresh_expo = jnp.exp(fresh - top)
        total = jnp.sum(expo, axis=1, keepdims=True) + fresh_expo
        probs = expo / total
        fresh_prob = jnp.where(own_mask, fresh_expo / total, 0.0).astype(BF)
        mixed = []
        for i in range(BLOCK // 2):
            values = vbuf[pl.ds(r0 + 2 * i, 2)].reshape(2 * SLOTS, DIM)
            first = jnp.concatenate([probs[16 * i : 16 * i + 8], blank], axis=1)
            second = jnp.concatenate([blank, probs[16 * i + 8 : 16 * i + 16]], axis=1)
            mixed.append(mm(jnp.concatenate([first, second], axis=0).astype(BF), values))
        oscr[part] = jnp.concatenate(mixed, axis=0) + mm(fresh_prob, nv[rows, :])
        for h in range(HEADS):
            att[rows, h * DIM : (h + 1) * DIM] = oscr[part, pl.ds(h, BLOCK, stride=HEADS), :].astype(BF)

    def send(src, dst, s, r, device):
        copy = pltpu.make_async_remote_copy(
            src_ref=src, dst_ref=dst, send_sem=s, recv_sem=r, device_id=device, device_id_type=MESH
        )
        copy.start()
        return copy

    tile = 512

    def ring(d, stage):
        return send(
            rs_send.at[d, stage], rs_recv.at[d, stage], s_rs.at[d, stage], r_rs.at[d, stage],
            to_tp(1 if d == 0 else 3),
        )

    def to_send(d, stage, start):
        def store(column, value):
            rs_send[d, stage, :, pl.ds(pl.multiple_of(column - start, tile), tile)] = value.astype(BF)

        return store

    def to_hold(d, start):
        def store(column, value):
            hold[d, :, pl.ds(pl.multiple_of(column - start, tile), tile)] = value

        return store

    def to_own(column, value):
        own[:, pl.ds(column, tile)] = value

    half = HALF // tile
    weights_done = [False] * TP

    def part(i, first, last, store):
        if not weights_done[i]:
            weights[i].wait()
            weights_done[i] = True

        def step(j, carry):
            column = pl.multiple_of(j * tile, tile)
            store(column, mm(att[...], wbuf[i, :, pl.ds(column, tile)]))
            return carry

        lax.fori_loop(first, last, step, 0)

    sent = [[None] * 3 for _ in range(2)]
    sent_half = [None, None]

    def ring_half(d, part_of):
        rows = pl.ds(part_of * (ROWS // 2), ROWS // 2)
        slot_of = 0 if part_of else 3
        return send(
            rs_send.at[d, 0, rows], rs_recv.at[d, 0, rows], s_rs.at[d, slot_of], r_rs.at[d, slot_of],
            to_tp(1 if d == 0 else 3),
        )

    def opposite(part_of):
        if part_of == 0:
            weights[0].wait()
        rows = slice(part_of * (ROWS // 2), (part_of + 1) * (ROWS // 2))
        for d in range(2):
            for j in range(half):
                columns = slice(j * tile, (j + 1) * tile)
                value = mm(att[rows, :], wbuf[0, :, d * HALF + j * tile : d * HALF + (j + 1) * tile])
                rs_send[d, 0, rows, columns] = value.astype(BF)
            copy = ring_half(d, part_of)
            if part_of:
                sent[d][0] = copy
            else:
                sent_half[d] = copy

    def kv_step(i, carry):
        for copy in kv_copies(i):
            copy.wait()

        @pl.when(i < KV_CHUNKS - KV_AHEAD)
        def _():
            start_kv(i + KV_AHEAD)

        @pl.when(i == W_AFTER)
        def _():
            weights[0].start()

        @pl.when(i == KV_CHUNKS - KV_AHEAD)
        def _():
            shrink_copy.start()

        r0 = pl.multiple_of(i * KV_ROWS, KV_ROWS)
        for part in range(KV_ROWS // BLOCK):
            attend(pl.multiple_of(r0 + part * BLOCK, BLOCK), part)
        return carry

    lax.fori_loop(0, KV_CHUNKS // 2, kv_step, 0)
    pl.semaphore_wait(barrier, PEERS - 1 + TP - 1)
    opposite(0)
    lax.fori_loop(KV_CHUNKS // 2, KV_CHUNKS, kv_step, 0)

    packed[:, :, :WIDTH] = mm(sel[...], att[...]).astype(BF).reshape(PEERS, CAP, WIDTH)
    fwd = [None] * PEERS
    for k in [q * QPEERS + j for q in range(QUARTERS) for j in ORDER][:PEERS]:
        if k == 0:
            continue
        fwd[k] = send(packed.at[k], arrived.at[k], s_fwd.at[k], r_fwd.at[k], to_ad(OFFSETS[k], 1))
    weights[1].start()
    arrived[0] = packed[0]

    opposite(1)
    weights[2].start()
    expand_copy.start()
    weights[3].start()
    part(1, half, 2 * half, to_send(0, 1, HALF))
    part(1, 0, half, to_hold(0, 0))
    shrink_copy.wait()
    expand_copy.wait()

    spread_mask = (iota((AUX, HELD * RANK), 0) == iota((AUX, HELD * RANK), 1) // RANK).astype(F32).astype(BF)
    low = iota((QROWS // 2, 2 * RANK), 1) < RANK
    ar = [None] * QUARTERS
    back = [None] * PEERS

    def down(g):
        for k in range(g * QPEERS, (g + 1) * QPEERS):
            if k:
                fwd[k].wait_recv()
        rows = arrived[g * QPEERS : (g + 1) * QPEERS].reshape(QROWS, PACK)
        full = mm(rows[:, :WIDTH], shrink[...])
        pick = mm(rows[:, WIDTH:], spread_mask)
        picks[g] = pick.astype(BF)
        kept = jnp.where(pick > 0.5, full, 0.0)
        folded = sum(kept[:, i * 128 : (i + 1) * 128] for i in range(HELD * RANK // 128))
        both = folded + pltpu.roll(folded, RANK, 1)
        half_rows = jnp.where(low, both[: QROWS // 2], both[QROWS // 2 :])
        ar_own[g] = half_rows
        ar_send[g] = half_rows.astype(BF)
        ar[g] = [
            send(ar_send.at[g], ar_recv.at[g, d], s_ar.at[g, d], r_ar.at[g, d], to_tp(d + 1))
            for d in range(TP - 1)
        ]

    def up(g):
        for copy in ar[g]:
            copy.wait()
        total = ar_own[g]
        for d in range(TP - 1):
            total = total + ar_recv[g, d].astype(F32)
        other = pltpu.roll(total, RANK, 1)
        both = jnp.concatenate([jnp.where(low, total, other), jnp.where(low, other, total)], axis=0).astype(BF)
        spread = jnp.concatenate([both] * (HELD * RANK // 128), axis=1) * picks[g]
        peers = slice(g * QPEERS, (g + 1) * QPEERS)
        for j in range(CHUNK // tile):
            columns = slice(j * tile, (j + 1) * tile)
            wid[peers, :, columns] = mm(spread, expand[:, columns]).astype(BF).reshape(QPEERS, CAP, tile)
        for k in range(g * QPEERS, (g + 1) * QPEERS):
            if k:
                back[k] = send(wid.at[k], ret.at[k], s_back.at[k], r_back.at[k], to_ad(OFFSETS[k], -1))
            else:
                ret[0] = wid[0]

    down(0)
    part(2, 0, half, to_send(1, 1, 0))
    part(2, half, 2 * half, to_hold(1, HALF))
    down(1)
    sent[0][1] = ring(0, 1)
    sent[1][1] = ring(1, 1)
    part(3, 0, 2 * half, to_own)
    down(2)
    up(0)
    up(1)
    down(3)
    for d in range(2):
        sent_half[d].wait_recv()
        sent[d][0].wait_recv()
        rs_send[d, 2] = (hold[d] + rs_recv[d, 0].astype(F32)).astype(BF)
        sent[d][2] = ring(d, 2)
    up(2)
    up(3)

    for d in range(2):
        sent[d][1].wait_recv()
    own[:, :HALF] += rs_recv[1, 1].astype(F32)
    own[:, HALF:] += rs_recv[0, 1].astype(F32)

    def returned(g, last=False):
        for k in range(g * QPEERS, (g + 1) * QPEERS):
            if k:
                back[k].wait_recv()
        chosen = sel_t[:, g * QROWS : (g + 1) * QROWS]
        for j in range(CHUNK // tile):
            columns = slice(j * tile, (j + 1) * tile)
            values = ret[g * QPEERS : (g + 1) * QPEERS, :, columns].reshape(QROWS, tile)
            value = own[:, columns] + mm(chosen, values)
            if last:
                out_ref[:, columns] = value.astype(BF)
            else:
                own[:, columns] = value

    returned(0)
    returned(1)
    for d in range(2):
        sent[d][2].wait_recv()
    own[:, :HALF] += rs_recv[0, 2].astype(F32)
    own[:, HALF:] += rs_recv[1, 2].astype(F32)
    returned(2)
    returned(3, last=True)

    for k in range(1, PEERS):
        fwd[k].wait_send()
        back[k].wait_send()
    for d in range(2):
        sent_half[d].wait_send()
        for stage in range(3):
            sent[d][stage].wait_send()


def shards(
    queries,
    key_cache,
    value_cache,
    new_key,
    new_value,
    lengths,
    out_weight,
    shrink_weight,
    expand_weight,
    adapter_id,
    adapter_slot,
):
    dma = pltpu.SemaphoreType.DMA
    hbm = pl.BlockSpec(memory_space=pl.ANY)
    vmem = pl.BlockSpec(memory_space=pltpu.VMEM)
    return pl.pallas_call(
        kernel,
        out_shape=pltpu.VMEM((ROWS, CHUNK), BF),
        in_specs=[hbm] * 11,
        out_specs=vmem,
        scratch_shapes=[
            pltpu.SMEM((ROWS,), jnp.int32),
            pltpu.VMEM((1, ROWS), jnp.int32),
            pltpu.VMEM((1, ROWS), jnp.int32),
            pltpu.VMEM((ROWS, WIDTH), BF),
            pltpu.VMEM((ROWS, SLOTS, DIM), BF),
            pltpu.VMEM((ROWS, SLOTS, DIM), BF),
            pltpu.VMEM((ROWS, DIM), BF),
            pltpu.VMEM((ROWS, DIM), BF),
            pltpu.VMEM((TP, WIDTH, CHUNK), BF),
            pltpu.VMEM((WIDTH, HELD * RANK), BF),
            pltpu.VMEM((HELD * RANK, CHUNK), BF),
            pltpu.VMEM((KV_ROWS // BLOCK, BLOCK * HEADS, DIM), F32),
            pltpu.VMEM((KV_ROWS // BLOCK, BLOCK * HEADS, DIM), F32),
            pltpu.VMEM((ROWS, WIDTH), BF),
            pltpu.VMEM((PEERS * CAP, ROWS), BF),
            pltpu.VMEM((ROWS, PEERS * CAP), BF),
            pltpu.VMEM((PEERS, CAP, PACK), BF),
            pltpu.VMEM((PEERS, CAP, PACK), BF),
            pltpu.VMEM((PEERS, CAP, CHUNK), BF),
            pltpu.VMEM((PEERS, CAP, CHUNK), BF),
            pltpu.VMEM((QUARTERS, QROWS, HELD * RANK), BF),
            pltpu.VMEM((QUARTERS, QROWS // 2, 2 * RANK), F32),
            pltpu.VMEM((QUARTERS, QROWS // 2, 2 * RANK), BF),
            pltpu.VMEM((QUARTERS, TP - 1, QROWS // 2, 2 * RANK), BF),
            pltpu.VMEM((2, 3, ROWS, HALF), BF),
            pltpu.VMEM((2, 3, ROWS, HALF), BF),
            pltpu.VMEM((2, ROWS, HALF), F32),
            pltpu.VMEM((ROWS, CHUNK), F32),
            dma((8,)),
            dma((KV_CHUNKS,)),
            dma((KV_CHUNKS,)),
            dma((TP,)),
            dma((PEERS,)),
            dma((PEERS,)),
            dma((PEERS,)),
            dma((PEERS,)),
            dma((QUARTERS, TP - 1)),
            dma((QUARTERS, TP - 1)),
            dma((2, 4)),
            dma((2, 4)),
        ],
        compiler_params=pltpu.CompilerParams(
            collective_id=0, has_side_effects=True, vmem_limit_bytes=58 * 2**20
        ),
    )(
        queries,
        key_cache,
        value_cache,
        new_key,
        new_value,
        out_weight,
        shrink_weight,
        expand_weight,
        lengths,
        adapter_id.reshape(1, ROWS),
        adapter_slot.reshape(1, ROWS),
    )


def solution(mesh):
    in_specs = (
        P("ad", "tp"),
        P("ad", None, "tp"),
        P("ad", None, "tp"),
        P("ad", "tp"),
        P("ad", "tp"),
        P("ad"),
        P("tp", None),
        P("tp", "ad"),
        P("ad", "tp"),
        P("ad"),
        P(),
    )
    out_specs = P("ad", "tp")
    return jax.shard_map(shards, mesh=mesh, in_specs=in_specs, out_specs=out_specs, check_vma=False)
```
